512 devices in a mesh: dp: 16 (over y, core), code: 32 (over x, z).
Axes of the slice: x: 4, y: 8, z: 8, core: 2. Of those that a mesh axis runs over, the one named last changes fastest.
Arguments:
- latents: bfloat16 [8192, 256], P('dp')
- upstream: bfloat16 [8192, 256], P('dp'), may hold values from -6 to 6
- targets: int32 [8192], P('dp'), may hold values from 0 to 131071
- codebook: bfloat16 [131072, 256], P('code')
Outputs:
- latent_grad: float32 [8192, 256], P('dp')
- codebook_grad: float32 [131072, 256], P(('code', 'dp'))
The draws below stay inside these ranges and needn't reach their ends.
All inputs are finite; a program needn't handle non-finite values.
Results may differ from the reference program's by a relative error of at most 0.0013.
Values sent between devices are 32-bit elements; how exact they have to be, the bound alone decides.
No kernel may reach another device: no remote copies, remote signals or barrier semaphores. Data moves between devices by JAX's collectives and lax.ppermute only.
A program may use at most 64 MiB of HBM per device.

```python
import math
import jax
import jax.numpy as jnp
from jax import lax

D = 256
K = 131072
ROWS = 8192


def shared_book(key):
    return jax.random.normal(key, (K, D), jnp.float32) * (3.0 / math.sqrt(D))


def draw_codebook(key, part):
    book = shared_book(key)
    return book.astype(jnp.bfloat16)


def draw_latents(key, part):
    key = jax.random.fold_in(key, 2)
    first = jax.random.fold_in(key, 0)
    values = jax.random.normal(first, (ROWS, D), jnp.float32)
    return values.astype(jnp.bfloat16)


def set_ends(drawn, rng, low, largest):
    index_at = [jax.random.randint(jax.random.fold_in(rng, axis), (), 0, length) for axis, length in enumerate(drawn.shape)]
    longest = drawn.shape.index(max(drawn.shape))
    beside = index_at[:longest] + [(index_at[longest] + 1) % drawn.shape[longest]] + index_at[longest + 1:]
    return drawn.at[tuple(index_at)].set(low).at[tuple(beside)].set(largest)


def block_scale(key, dims, pieces, least, high):
    level, own = 1.0, jax.random.fold_in(key, 6)
    for position, parts in pieces:
        draws = jnp.exp(jax.random.uniform(jax.random.fold_in(own, position), (parts,), jnp.float32, least / len(pieces), high / len(pieces)))
        level = level * jnp.repeat(draws, dims[position] // parts).reshape([-1 if axis == position else 1 for axis in range(len(dims))])
    return level


def noise(stream_key, shape, scale, limit, cuts=(), kind=jnp.bfloat16):
    entries = jax.random.normal(stream_key, shape, jnp.float32) * scale
    if len(cuts) > 0:
        entries = block_scale(stream_key, shape, cuts, -0.22, 0.18) * entries
    return jnp.clip(entries, min=-limit, max=limit).astype(kind)


def setup_inputs(seed: int = 0) -> dict:
    streams_of = jax.random.split(jax.random.key(seed), 5)
    return {
        "latents": draw_latents(jax.random.fold_in(streams_of[4], 71), 0),
        "upstream": noise(streams_of[1], (ROWS, D), 1.0, 6.0, ((0, 16),)),
        "targets": set_ends(jax.random.randint(streams_of[2], (ROWS,), 0, K), jax.random.fold_in(streams_of[2], 1), 0, K - 1).astype(jnp.int32),
        "codebook": draw_codebook(jax.random.fold_in(streams_of[4], 71), 0),
    }


def reference(latents, upstream, targets, codebook):
    block = min(256, ROWS)
    count = ROWS // block
    lat_blocks = latents.reshape(count, block, D)
    up_blocks = upstream.reshape(count, block, D)
    tgt_blocks = targets.reshape(count, block)
    book_t = codebook.T
    columns = jnp.arange(K, dtype=jnp.int32)

    def step(total, item):
        lat, grad_up, tgt = item
        scores = jnp.dot(lat, book_t, preferred_element_type=jnp.float32)
        dprob = jnp.dot(grad_up, book_t, preferred_element_type=jnp.float32)
        top = jnp.max(scores, axis=1, keepdims=True)
        expo = jnp.exp(scores - top)
        probs = expo / jnp.sum(expo, axis=1, keepdims=True)
        rowdot = jnp.sum(probs * dprob, axis=1, keepdims=True)
        onehot = (columns[None, :] == tgt[:, None]).astype(jnp.float32)
        dscore = (probs * (dprob - rowdot) + probs - onehot).astype(jnp.bfloat16)
        probs_low = probs.astype(jnp.bfloat16)
        lat_grad = jnp.dot(dscore, codebook, preferred_element_type=jnp.float32)
        total = total + jnp.dot(dscore.T, lat, preferred_element_type=jnp.float32)
        total = total + jnp.dot(probs_low.T, grad_up, preferred_element_type=jnp.float32)
        return total, lat_grad

    total, lat_grads = lax.scan(step, jnp.zeros((K, D), jnp.float32), (lat_blocks, up_blocks, tgt_blocks))
    return lat_grads.reshape(ROWS, D), total
```

```python
import jax
import jax.numpy as jnp
from jax import lax
from jax.sharding import PartitionSpec as P


def shards(latents, upstream, targets, codebook):
    rows, width = latents.shape
    local_codes = codebook.shape[0]
    n_code = lax.axis_size("code")
    n_dp = lax.axis_size("dp")
    contract = (((1,), (1,)), ((), ()))
    scores = lax.dot_general(latents, codebook, contract, preferred_element_type=jnp.float32)
    dprob = lax.dot_general(upstream, codebook, contract, preferred_element_type=jnp.float32)
    top = jnp.max(scores, axis=1)
    expo = jnp.exp(scores - top[:, None])
    stats = jnp.stack([top, jnp.sum(expo, axis=1), jnp.sum(expo * dprob, axis=1)])
    every = lax.all_to_all(
        jnp.broadcast_to(stats[None], (n_code,) + stats.shape), "code", 0, 0
    )
    tops = every[:, 0]
    share = jnp.exp(tops - jnp.max(tops, axis=0)[None])
    total = jnp.sum(share * every[:, 1], axis=0)
    rowdot = jnp.sum(share * every[:, 2], axis=0) / total
    scale = jnp.exp(top - jnp.max(tops, axis=0)) / total
    probs = expo * scale[:, None]
    local_target = targets - lax.axis_index("code") * local_codes
    columns = lax.broadcasted_iota(jnp.int32, (rows, local_codes), 1)
    soft_part = probs * (dprob - rowdot[:, None]) + probs
    dscore = jnp.where(columns == local_target[:, None], soft_part - 1.0, soft_part).astype(
        jnp.bfloat16
    )
    probs_low = probs.astype(jnp.bfloat16)
    left = jnp.concatenate([dscore, probs_low], axis=0)
    stacked = jnp.concatenate([latents, upstream], axis=0)
    term = lax.dot_general(
        left, stacked, (((0,), (0,)), ((), ())), preferred_element_type=jnp.float32
    )
    chips = n_dp // 2
    term = term.reshape(chips, 2, local_codes // n_dp, width)
    core = lax.rem(lax.axis_index("dp"), 2)
    mine = lax.dynamic_index_in_dim(term, core, 1, keepdims=False)
    other = lax.dynamic_index_in_dim(term, 1 - core, 1, keepdims=False)
    got = lax.ppermute(other, "dp", [(i, i ^ 1) for i in range(n_dp)])
    half = (mine + got).reshape(local_codes // 2, width)
    groups = [[2 * y + c for y in range(chips)] for c in range(2)]
    codebook_grad = lax.psum_scatter(
        half, "dp", scatter_dimension=0, axis_index_groups=groups, tiled=True
    )
    lat_part = jnp.dot(dscore, codebook, preferred_element_type=jnp.float32)
    pieces = lax.all_to_all(
        lat_part.reshape(n_code, rows // n_code, width), "code", 0, 0
    )
    piece = jnp.sum(pieces, axis=0)
    latent_grad = lax.all_to_all(
        jnp.broadcast_to(piece[None], (n_code,) + piece.shape), "code", 0, 0
    ).reshape(rows, width)
    return (latent_grad, codebook_grad)


def solution(mesh):
    return jax.shard_map(
        shards,
        mesh=mesh,
        in_specs=(P("dp", None), P("dp", None), P("dp"), P("code", None)),
        out_specs=(P("dp", None), P(("code", "dp"), None)),
        check_vma=False,
    )
```

```python
import functools

import jax
import jax.numpy as jnp
from jax import lax
from jax.experimental import pallas as pl
from jax.experimental.pallas import tpu as pltpu
from jax.sharding import PartitionSpec as P

ROW_CONTRACT = (((1,), (1,)), ((), ()))
CODE_CONTRACT = (((0,), (0,)), ((), ()))
VMEM = pl.BlockSpec(memory_space=pltpu.VMEM)
SMEM = pl.BlockSpec(memory_space=pltpu.SMEM)
PARAMS = pltpu.CompilerParams(vmem_limit_bytes=40 * 1024 * 1024)


def dot(a, b, contract):
    return lax.dot_general(a, b, contract, preferred_element_type=jnp.float32)


def stats_kernel(tile, lat_ref, up_ref, book_ref, out_ref):
    lat, up = lat_ref[...], up_ref[...]
    tops, totals, weights = [], [], []
    for start in range(0, book_ref.shape[0], tile):
        book = book_ref[start : start + tile, :]
        scores = dot(book, lat, ROW_CONTRACT)
        dprob = dot(book, up, ROW_CONTRACT)
        top = jnp.max(scores, axis=0, keepdims=True)
        expo = jnp.exp(scores - top)
        tops.append(top)
        totals.append(jnp.sum(expo, axis=0, keepdims=True))
        weights.append(jnp.sum(expo * dprob, axis=0, keepdims=True))
    top = functools.reduce(jnp.maximum, tops)
    shares = [jnp.exp(t - top) for t in tops]
    total = sum(s * t for s, t in zip(shares, totals))
    weight = sum(s * w for s, w in zip(shares, weights))
    stats = jnp.concatenate([top, total, weight], axis=0)
    out_ref[...] = jnp.broadcast_to(stats[None], out_ref.shape)


def half_kernel(chunk, where_ref, row_ref, target_ref, lat_ref, up_ref, book_ref, grad_ref, dscore_ref):
    lat, up = lat_ref[...], up_ref[...]
    top, inverse, shift = row_ref[0:1, :], row_ref[1:2, :], row_ref[2:3, :]
    target = target_ref[...]
    codes = lax.broadcasted_iota(jnp.int32, (chunk, lat.shape[0]), 0)
    for pair in range(grad_ref.shape[0] // chunk):
        start = pl.multiple_of((2 * pair + where_ref[0]) * chunk, chunk)
        book = book_ref[pl.ds(start, chunk), :]
        scores = dot(book, lat, ROW_CONTRACT)
        dprob = dot(book, up, ROW_CONTRACT)
        probs = jnp.exp(scores - top) * inverse
        soft = probs * (dprob + shift)
        dscore = jnp.where(codes == target - start, soft - 1.0, soft).astype(jnp.bfloat16)
        here = slice(pair * chunk, (pair + 1) * chunk)
        dscore_ref[here, :] = dscore
        grad_ref[here, :] = dot(dscore, lat, (((1,), (0,)), ((), ()))) + dot(
            probs.astype(jnp.bfloat16), up, (((1,), (0,)), ((), ()))
        )


def latent_kernel(chunk, where_ref, mine_ref, other_ref, book_ref, out_ref):
    total = jnp.zeros((book_ref.shape[1], mine_ref.shape[1]), jnp.float32)
    for pair in range(mine_ref.shape[0] // chunk):
        here = slice(pair * chunk, (pair + 1) * chunk)
        for dscore_ref, side in ((mine_ref, where_ref[0]), (other_ref, 1 - where_ref[0])):
            start = pl.multiple_of((2 * pair + side) * chunk, chunk)
            total += dot(book_ref[pl.ds(start, chunk), :], dscore_ref[here, :], CODE_CONTRACT)
    out_ref[...] = total.T


def shards(latents, upstream, targets, codebook):
    rows, width = latents.shape
    local_codes = codebook.shape[0]
    n_code = lax.axis_size("code")
    n_dp = lax.axis_size("dp")
    chips = n_dp // 2
    chunk = local_codes // n_dp
    core = lax.rem(lax.axis_index("dp"), 2)
    macs = rows * local_codes * width
    f32, bf16 = jnp.float32, jnp.bfloat16

    stats = pl.pallas_call(
        functools.partial(stats_kernel, 512),
        out_shape=jax.ShapeDtypeStruct((n_code, 3, rows), f32),
        in_specs=[VMEM] * 3,
        out_specs=VMEM,
        compiler_params=PARAMS,
        cost_estimate=pl.CostEstimate(
            flops=4 * macs, bytes_accessed=3 << 20, transcendentals=rows * local_codes
        ),
        name="stats",
    )(latents, upstream, codebook)
    every = lax.all_to_all(stats, "code", 0, 0)
    tops = every[:, 0]
    top = jnp.max(tops, axis=0)
    share = jnp.exp(tops - top[None])
    total = jnp.sum(share * every[:, 1], axis=0)
    rowdot = jnp.sum(share * every[:, 2], axis=0) / total
    row = jnp.stack([top, 1.0 / total, 1.0 - rowdot])
    local_target = (targets - lax.axis_index("code") * local_codes)[None]

    half_call = pl.pallas_call(
        functools.partial(half_kernel, chunk),
        out_shape=(
            jax.ShapeDtypeStruct((local_codes // 2, width), f32),
            jax.ShapeDtypeStruct((local_codes // 2, rows), bf16),
        ),
        in_specs=[SMEM] + [VMEM] * 5,
        out_specs=(VMEM, VMEM),
        compiler_params=PARAMS,
        cost_estimate=pl.CostEstimate(
            flops=4 * macs, bytes_accessed=6 << 20, transcendentals=rows * local_codes // 2
        ),
        name="codebook_half",
    )
    away = half_call((1 - core)[None], row, local_target, latents, upstream, codebook)
    got = lax.ppermute(away[0], "dp", [(i, i ^ 1) for i in range(n_dp)])
    mine = half_call(core[None], row, local_target, latents, upstream, codebook)
    groups = [[2 * y + c for y in range(chips)] for c in range(2)]
    codebook_grad = lax.psum_scatter(
        mine[0] + got, "dp", scatter_dimension=0, axis_index_groups=groups, tiled=True
    )
    lat_part = pl.pallas_call(
        functools.partial(latent_kernel, chunk),
        out_shape=jax.ShapeDtypeStruct((rows, width), f32),
        in_specs=[SMEM] + [VMEM] * 3,
        out_specs=VMEM,
        compiler_params=PARAMS,
        cost_estimate=pl.CostEstimate(flops=2 * macs, bytes_accessed=7 << 20, transcendentals=0),
        name="latent_part",
    )(core[None], mine[1], away[1], codebook)
    pieces = lax.all_to_all(lat_part.reshape(n_code, rows // n_code, width), "code", 0, 0)
    piece = jnp.sum(pieces, axis=0)
    latent_grad = lax.all_to_all(
        jnp.broadcast_to(piece[None], (n_code,) + piece.shape), "code", 0, 0
    ).reshape(rows, width)
    return (latent_grad, codebook_grad)


def solution(mesh):
    return jax.shard_map(
        shards,
        mesh=mesh,
        in_specs=(P("dp", None), P("dp", None), P("dp"), P("code", None)),
        out_specs=(P("dp", None), P(("code", "dp"), None)),
        check_vma=False,
    )
```

```python
import functools

import jax
import jax.numpy as jnp
from jax import lax
from jax.experimental import pallas as pl
from jax.experimental.pallas import tpu as pltpu
from jax.sharding import PartitionSpec as P

ROW_CONTRACT = (((1,), (1,)), ((), ()))
CODE_CONTRACT = (((0,), (0,)), ((), ()))
PLAIN = (((1,), (0,)), ((), ()))
VMEM = pl.BlockSpec(memory_space=pltpu.VMEM)
SMEM = pl.BlockSpec(memory_space=pltpu.SMEM)
HBM = pl.BlockSpec(memory_space=pltpu.HBM)
PARAMS = pltpu.CompilerParams(vmem_limit_bytes=24 * 1024 * 1024)


def dot(a, b, contract):
    return lax.dot_general(a, b, contract, preferred_element_type=jnp.float32)


def stats_kernel(tile, lat_hbm, up_hbm, book_hbm, out_ref, lat_ref, up_ref, book_ref, sems):
    starts = range(0, book_hbm.shape[0], tile)
    loads = [pltpu.make_async_copy(lat_hbm, lat_ref, sems.at[0])]
    for n, start in enumerate(starts):
        part = pl.ds(start, tile)
        loads.append(pltpu.make_async_copy(book_hbm.at[part], book_ref.at[part], sems.at[n + 1]))
    loads.insert(2, pltpu.make_async_copy(up_hbm, up_ref, sems.at[len(loads)]))
    for load in loads:
        load.start()
    loads[0].wait()
    tops, totals, weights = [], [], []
    for n, start in enumerate(starts):
        if n == 0:
            loads[1].wait()
            loads[2].wait()
        else:
            loads[n + 2].wait()
        book = book_ref[start : start + tile, :]
        scores = dot(book, lat_ref[...], ROW_CONTRACT)
        dprob = dot(book, up_ref[...], ROW_CONTRACT)
        top = jnp.max(scores, axis=0, keepdims=True)
        expo = jnp.exp(scores - top)
        tops.append(top)
        totals.append(jnp.sum(expo, axis=0, keepdims=True))
        weights.append(jnp.sum(expo * dprob, axis=0, keepdims=True))
    top = functools.reduce(jnp.maximum, tops)
    shares = [jnp.exp(t - top) for t in tops]
    total = sum(s * t for s, t in zip(shares, totals))
    weight = sum(s * w for s, w in zip(shares, weights))
    stats = jnp.concatenate([top, total, weight], axis=0)
    out_ref[...] = jnp.broadcast_to(stats[None], out_ref.shape)


def chunk_ids(chips, y, core):
    step = 1 - 2 * core
    ids = []
    for far in range(1, chips // 2):
        chip = lax.rem(y + far * step + chips, chips)
        ids += [2 * chip + core, 2 * chip + 1 - core]
    return ids + [2 * lax.rem(y + chips // 2, chips) + core, 2 * y + core]


def half_kernel(chunk, where_ref, row_ref, target_ref, lat_ref, up_ref, book_ref, grad_ref, dscore_ref):
    lat, up = lat_ref[...], up_ref[...]
    top, inverse, shift = row_ref[0:1, :], row_ref[1:2, :], row_ref[2:3, :]
    target = target_ref[...]
    codes = lax.broadcasted_iota(jnp.int32, (chunk, lat.shape[0]), 0)
    ids = chunk_ids(book_ref.shape[0] // chunk // 2, where_ref[0], where_ref[1])
    for n, which in enumerate(ids):
        start = pl.multiple_of(which * chunk, chunk)
        book = book_ref[pl.ds(start, chunk), :]
        scores = dot(book, lat, ROW_CONTRACT)
        dprob = dot(book, up, ROW_CONTRACT)
        probs = jnp.exp(scores - top) * inverse
        soft = probs * (dprob + shift)
        dscore = jnp.where(codes == target - start, soft - 1.0, soft).astype(jnp.bfloat16)
        here = slice(n * chunk, (n + 1) * chunk)
        dscore_ref[here, :] = dscore
        grad_ref[here, :] = dot(dscore, lat, PLAIN) + dot(probs.astype(jnp.bfloat16), up, PLAIN)


def latent_kernel(chunk, where_ref, mine_ref, other_ref, book_ref, out_ref):
    total = jnp.zeros((book_ref.shape[1], mine_ref.shape[1]), jnp.float32)
    chips = book_ref.shape[0] // chunk // 2
    for dscore_ref, core in ((mine_ref, where_ref[1]), (other_ref, 1 - where_ref[1])):
        for n, which in enumerate(chunk_ids(chips, where_ref[0], core)):
            start = pl.multiple_of(which * chunk, chunk)
            here = slice(n * chunk, (n + 1) * chunk)
            total += dot(book_ref[pl.ds(start, chunk), :], dscore_ref[here, :], CODE_CONTRACT)
    out_ref[...] = total.T


def shards(latents, upstream, targets, codebook):
    rows, width = latents.shape
    local_codes = codebook.shape[0]
    n_code = lax.axis_size("code")
    n_dp = lax.axis_size("dp")
    chips = n_dp // 2
    chunk = local_codes // n_dp
    here = lax.axis_index("dp")
    y, core = here // 2, lax.rem(here, 2)
    macs = rows * local_codes * width
    f32, bf16 = jnp.float32, jnp.bfloat16

    tile = 512
    stats = pl.pallas_call(
        functools.partial(stats_kernel, tile),
        out_shape=jax.ShapeDtypeStruct((n_code, 3, rows), f32),
        in_specs=[HBM] * 3,
        out_specs=VMEM,
        scratch_shapes=[
            pltpu.VMEM((rows, width), bf16),
            pltpu.VMEM((rows, width), bf16),
            pltpu.VMEM((local_codes, width), bf16),
            pltpu.SemaphoreType.DMA((local_codes // tile + 2,)),
        ],
        compiler_params=pltpu.CompilerParams(vmem_limit_bytes=60 * 1024 * 1024),
        cost_estimate=pl.CostEstimate(
            flops=4 * macs, bytes_accessed=3 << 20, transcendentals=rows * local_codes
        ),
        name="stats",
    )(latents, upstream, codebook)
    every = lax.all_to_all(stats, "code", 0, 0)
    tops = every[:, 0]
    top = jnp.max(tops, axis=0)
    share = jnp.exp(tops - top[None])
    total = jnp.sum(share * every[:, 1], axis=0)
    rowdot = jnp.sum(share * every[:, 2], axis=0) / total
    row = jnp.stack([top, 1.0 / total, 1.0 - rowdot])
    local_target = (targets - lax.axis_index("code") * local_codes)[None]

    half_call = pl.pallas_call(
        functools.partial(half_kernel, chunk),
        out_shape=(
            jax.ShapeDtypeStruct((local_codes // 2, width), f32),
            jax.ShapeDtypeStruct((local_codes // 2, rows), bf16),
        ),
        in_specs=[SMEM] + [VMEM] * 5,
        out_specs=(VMEM, VMEM),
        compiler_params=PARAMS,
        cost_estimate=pl.CostEstimate(
            flops=4 * macs, bytes_accessed=6 << 20, transcendentals=rows * local_codes // 2
        ),
        name="codebook_half",
    )
    away = half_call(jnp.stack([y, 1 - core]), row, local_target, latents, upstream, codebook)
    got = lax.ppermute(away[0], "dp", [(i, i ^ 1) for i in range(n_dp)])
    mine = half_call(jnp.stack([y, core]), row, local_target, latents, upstream, codebook)
    lat_part = pl.pallas_call(
        functools.partial(latent_kernel, chunk),
        out_shape=jax.ShapeDtypeStruct((rows, width), f32),
        in_specs=[SMEM] + [VMEM] * 3,
        out_specs=VMEM,
        compiler_params=PARAMS,
        cost_estimate=pl.CostEstimate(flops=2 * macs, bytes_accessed=7 << 20, transcendentals=0),
        name="latent_part",
    )(jnp.stack([y, core]), mine[1], away[1], codebook)
    half, lat_part = lax.optimization_barrier((mine[0], lat_part))

    def along(far):
        return [
            (i, (i // 2 + far * (1 - 2 * (i % 2))) % chips * 2 + i % 2) for i in range(n_dp)
        ]

    near, middle, far, across, own = [
        half[at : at + size] + got[at : at + size]
        for at, size in (
            (0, 2 * chunk),
            (2 * chunk, 2 * chunk),
            (4 * chunk, 2 * chunk),
            (6 * chunk, chunk),
            (7 * chunk, chunk),
        )
    ]
    near, middle, far, across, own, lat_part = lax.optimization_barrier(
        (near, middle, far, across, own, lat_part)
    )
    far_came = lax.ppermute(far, "dp", along(1))
    across_came = lax.ppermute(across, "dp", along(2))
    near_came = lax.ppermute(near, "dp", along(1))
    merged = jnp.concatenate(
        [middle[:chunk] + far_came[:chunk] + across_came, middle[chunk:] + far_came[chunk:]]
    )
    merged_came = lax.ppermute(merged, "dp", along(2))

    pieces = lax.all_to_all(lat_part.reshape(n_code, rows // n_code, width), "code", 0, 0)
    piece = jnp.sum(pieces, axis=0)
    latent_grad = lax.all_to_all(
        jnp.broadcast_to(piece[None], (n_code,) + piece.shape), "code", 0, 0
    ).reshape(rows, width)

    last = lax.ppermute(
        near_came[chunk:] + merged_came[chunk:], "dp", [(i, i ^ 1) for i in range(n_dp)]
    )
    codebook_grad = near_came[:chunk] + merged_came[:chunk] + own + last
    return (latent_grad, codebook_grad)


def solution(mesh):
    return jax.shard_map(
        shards,
        mesh=mesh,
        in_specs=(P("dp", None), P("dp", None), P("dp"), P("code", None)),
        out_specs=(P("dp", None), P(("code", "dp"), None)),
        check_vma=False,
    )
```

```python
import functools

import jax
import jax.numpy as jnp
from jax import lax
from jax.experimental import pallas as pl
from jax.experimental.pallas import tpu as pltpu
from jax.sharding import PartitionSpec as P

ROW_CONTRACT = (((1,), (1,)), ((), ()))
CODE_CONTRACT = (((0,), (0,)), ((), ()))
PLAIN = (((1,), (0,)), ((), ()))
VMEM = pl.BlockSpec(memory_space=pltpu.VMEM)
SMEM = pl.BlockSpec(memory_space=pltpu.SMEM)
HBM = pl.BlockSpec(memory_space=pltpu.HBM)
PARAMS = pltpu.CompilerParams(vmem_limit_bytes=24 * 1024 * 1024)


def dot(a, b, contract):
    return lax.dot_general(a, b, contract, preferred_element_type=jnp.float32)


def stats_kernel(tile, lat_hbm, up_hbm, book_hbm, out_ref, lat_ref, up_ref, book_ref, sems):
    parts = [pl.ds(start, tile) for start in range(0, book_hbm.shape[0], tile)]
    lat_load = pltpu.make_async_copy(lat_hbm, lat_ref, sems.at[len(parts)])
    up_load = pltpu.make_async_copy(up_hbm, up_ref, sems.at[len(parts) + 1])
    loads = [
        pltpu.make_async_copy(book_hbm.at[part], book_ref.at[part], sems.at[n])
        for n, part in enumerate(parts)
    ]
    for load in (lat_load, loads[0], up_load, *loads[1:]):
        load.start()
    lat_load.wait()
    tops, totals, weights = [], [], []
    for n, part in enumerate(parts):
        loads[n].wait()
        if n == 0:
            up_load.wait()
        book = book_ref[part, :]
        scores = dot(book, lat_ref[...], ROW_CONTRACT)
        dprob = dot(book, up_ref[...], ROW_CONTRACT)
        top = jnp.max(scores, axis=0, keepdims=True)
        expo = jnp.exp(scores - top)
        tops.append(top)
        totals.append(jnp.sum(expo, axis=0, keepdims=True))
        weights.append(jnp.sum(expo * dprob, axis=0, keepdims=True))
    top = functools.reduce(jnp.maximum, tops)
    shares = [jnp.exp(t - top) for t in tops]
    total = sum(s * t for s, t in zip(shares, totals))
    weight = sum(s * w for s, w in zip(shares, weights))
    stats = jnp.concatenate([top, total, weight], axis=0)
    out_ref[...] = jnp.broadcast_to(stats[None], out_ref.shape)


def chunk_ids(chips, y, core):
    step = 1 - 2 * core
    ids = []
    for far in range(1, chips // 2):
        chip = lax.rem(y + far * step + chips, chips)
        ids += [2 * chip + core, 2 * chip + 1 - core]
    return ids + [2 * lax.rem(y + chips // 2, chips) + core, 2 * y + core]


def half_step(chunk, start, row_ref, target_ref, lat_ref, up_ref, book_ref):
    lat, up = lat_ref[...], up_ref[...]
    book = book_ref[pl.ds(start, chunk), :]
    scores = dot(book, lat, ROW_CONTRACT)
    dprob = dot(book, up, ROW_CONTRACT)
    probs = jnp.exp(scores - row_ref[0:1, :]) * row_ref[1:2, :]
    soft = probs * (dprob + row_ref[2:3, :])
    codes = lax.broadcasted_iota(jnp.int32, soft.shape, 0)
    dscore = jnp.where(codes == target_ref[...] - start, soft - 1.0, soft).astype(jnp.bfloat16)
    return dscore, dot(dscore, lat, PLAIN) + dot(probs.astype(jnp.bfloat16), up, PLAIN)


def away_kernel(chunk, ids_ref, row_ref, target_ref, lat_ref, up_ref, book_ref, grad_ref, dscore_ref):
    half = grad_ref.shape[0] // chunk
    for n in range(half):
        start = pl.multiple_of(ids_ref[half + n] * chunk, chunk)
        here = slice(n * chunk, (n + 1) * chunk)
        dscore_ref[here, :], grad_ref[here, :] = half_step(
            chunk, start, row_ref, target_ref, lat_ref, up_ref, book_ref
        )


def mine_kernel(
    chunk, ids_ref, row_ref, target_ref, lat_ref, up_ref, book_ref, away_ref, grad_ref, out_ref
):
    total = jnp.zeros((book_ref.shape[1], lat_ref.shape[0]), jnp.float32)
    half = grad_ref.shape[0] // chunk
    for n in range(half):
        start = pl.multiple_of(ids_ref[n] * chunk, chunk)
        away_start = pl.multiple_of(ids_ref[half + n] * chunk, chunk)
        here = slice(n * chunk, (n + 1) * chunk)
        dscore, grad_ref[here, :] = half_step(
            chunk, start, row_ref, target_ref, lat_ref, up_ref, book_ref
        )
        total += dot(book_ref[pl.ds(start, chunk), :], dscore, CODE_CONTRACT)
        total += dot(book_ref[pl.ds(away_start, chunk), :], away_ref[here, :], CODE_CONTRACT)
    out_ref[...] = total.T


def merge_kernel(chunk, middle_ref, far_ref, across_ref, same_ref, cross_ref):
    same_ref[...] = middle_ref[:chunk, :] + far_ref[:chunk, :] + across_ref[...]
    cross_ref[...] = middle_ref[chunk:, :] + far_ref[chunk:, :]


def shards(latents, upstream, targets, codebook):
    rows, width = latents.shape
    local_codes = codebook.shape[0]
    n_code = lax.axis_size("code")
    n_dp = lax.axis_size("dp")
    chips = n_dp // 2
    chunk = local_codes // n_dp
    here = lax.axis_index("dp")
    y, core = here // 2, lax.rem(here, 2)
    macs = rows * local_codes * width
    f32, bf16 = jnp.float32, jnp.bfloat16

    tile = 1024
    stats = pl.pallas_call(
        functools.partial(stats_kernel, tile),
        out_shape=jax.ShapeDtypeStruct((n_code, 3, rows), f32),
        in_specs=[HBM] * 3,
        out_specs=VMEM,
        scratch_shapes=[
            pltpu.VMEM((rows, width), bf16),
            pltpu.VMEM((rows, width), bf16),
            pltpu.VMEM((local_codes, width), bf16),
            pltpu.SemaphoreType.DMA((local_codes // tile + 2,)),
        ],
        compiler_params=pltpu.CompilerParams(vmem_limit_bytes=60 * 1024 * 1024),
        cost_estimate=pl.CostEstimate(
            flops=4 * macs, bytes_accessed=3 << 20, transcendentals=rows * local_codes
        ),
        name="stats",
    )(latents, upstream, codebook)
    every = lax.all_to_all(stats, "code", 0, 0)
    tops = every[:, 0]
    top = jnp.max(tops, axis=0)
    share = jnp.exp(tops - top[None])
    total = jnp.sum(share * every[:, 1], axis=0)
    rowdot = jnp.sum(share * every[:, 2], axis=0) / total
    row = jnp.stack([top, 1.0 / total, 1.0 - rowdot])
    local_target = (targets - lax.axis_index("code") * local_codes)[None]

    ids = jnp.stack(chunk_ids(chips, y, core) + chunk_ids(chips, y, 1 - core))
    operands = (ids, row, local_target, latents, upstream, codebook)
    away, away_dscore = pl.pallas_call(
        functools.partial(away_kernel, chunk),
        out_shape=(
            jax.ShapeDtypeStruct((local_codes // 2, width), f32),
            jax.ShapeDtypeStruct((local_codes // 2, rows), bf16),
        ),
        in_specs=[SMEM] + [VMEM] * 5,
        out_specs=(VMEM, VMEM),
        compiler_params=PARAMS,
        cost_estimate=pl.CostEstimate(
            flops=4 * macs, bytes_accessed=6 << 20, transcendentals=rows * local_codes // 2
        ),
        name="away_half",
    )(*operands)
    got = lax.ppermute(away, "dp", [(i, i ^ 1) for i in range(n_dp)])
    half, lat_part = pl.pallas_call(
        functools.partial(mine_kernel, chunk),
        out_shape=(
            jax.ShapeDtypeStruct((local_codes // 2, width), f32),
            jax.ShapeDtypeStruct((rows, width), f32),
        ),
        in_specs=[SMEM] + [VMEM] * 6,
        out_specs=(VMEM, VMEM),
        compiler_params=PARAMS,
        cost_estimate=pl.CostEstimate(
            flops=6 * macs, bytes_accessed=7 << 20, transcendentals=rows * local_codes // 2
        ),
        name="mine_half",
    )(*operands, away_dscore)

    def along(far, other=0):
        return [
            (i, (i // 2 + far * (1 - 2 * (i % 2))) % chips * 2 + (i + other) % 2)
            for i in range(n_dp)
        ]

    *near, middle, far, across, own = [
        half[at : at + size] + got[at : at + size]
        for at, size in (
            (0, chunk),
            (chunk, chunk),
            (2 * chunk, 2 * chunk),
            (4 * chunk, 2 * chunk),
            (6 * chunk, chunk),
            (7 * chunk, chunk),
        )
    ]
    *near, middle, far, across, own, lat_part = lax.optimization_barrier(
        (*near, middle, far, across, own, lat_part)
    )
    far_came = lax.ppermute(far, "dp", along(1))
    across_came = lax.ppermute(across, "dp", along(2))
    near_came = [lax.ppermute(near[n], "dp", along(1, n)) for n in (0, 1)]
    merged = pl.pallas_call(
        functools.partial(merge_kernel, chunk),
        out_shape=[jax.ShapeDtypeStruct((chunk, width), f32)] * 2,
        in_specs=[VMEM] * 3,
        out_specs=[VMEM] * 2,
        compiler_params=PARAMS,
        cost_estimate=pl.CostEstimate(flops=6000000000, bytes_accessed=2 << 20, transcendentals=0),
        name="merge",
    )(middle, far_came, across_came)
    merged_came = [lax.ppermute(merged[n], "dp", along(2, n)) for n in (0, 1)]

    pieces = lax.all_to_all(lat_part.reshape(n_code, rows // n_code, width), "code", 0, 0)
    piece = jnp.sum(pieces, axis=0)
    latent_grad = lax.all_to_all(
        jnp.broadcast_to(piece[None], (n_code,) + piece.shape), "code", 0, 0
    ).reshape(rows, width)

    codebook_grad = near_came[0] + near_came[1] + merged_came[0] + merged_came[1] + own
    return (latent_grad, codebook_grad)


def solution(mesh):
    return jax.shard_map(
        shards,
        mesh=mesh,
        in_specs=(P("dp", None), P("dp", None), P("dp"), P("code", None)),
        out_specs=(P("dp", None), P(("code", "dp"), None)),
        check_vma=False,
    )
```

```python
import functools

import jax
import jax.numpy as jnp
from jax import lax
from jax.experimental import pallas as pl
from jax.experimental.pallas import tpu as pltpu
from jax.sharding import PartitionSpec as P

ROW_CONTRACT = (((1,), (1,)), ((), ()))
CODE_CONTRACT = (((0,), (0,)), ((), ()))
PLAIN = (((1,), (0,)), ((), ()))
VMEM = pl.BlockSpec(memory_space=pltpu.VMEM)
SMEM = pl.BlockSpec(memory_space=pltpu.SMEM)
HBM = pl.BlockSpec(memory_space=pltpu.HBM)
PARAMS = pltpu.CompilerParams(vmem_limit_bytes=24 * 1024 * 1024)


def dot(a, b, contract):
    return lax.dot_general(a, b, contract, preferred_element_type=jnp.float32)


def stats_kernel(tile, lat_hbm, up_hbm, book_hbm, out_ref, lat_ref, up_ref, book_ref, sems):
    parts = [pl.ds(start, tile) for start in range(0, book_hbm.shape[0], tile)]
    lat_load = pltpu.make_async_copy(lat_hbm, lat_ref, sems.at[len(parts)])
    up_load = pltpu.make_async_copy(up_hbm, up_ref, sems.at[len(parts) + 1])
    loads = [
        pltpu.make_async_copy(book_hbm.at[part], book_ref.at[part], sems.at[n])
        for n, part in enumerate(parts)
    ]
    for load in (lat_load, loads[0], up_load, *loads[1:]):
        load.start()
    lat_load.wait()
    tops, totals, weights = [], [], []
    for n, part in enumerate(parts):
        loads[n].wait()
        if n == 0:
            up_load.wait()
        book = book_ref[part, :]
        scores = dot(book, lat_ref[...], ROW_CONTRACT)
        dprob = dot(book, up_ref[...], ROW_CONTRACT)
        top = jnp.max(scores, axis=0, keepdims=True)
        expo = jnp.exp(scores - top)
        tops.append(top)
        totals.append(jnp.sum(expo, axis=0, keepdims=True))
        weights.append(jnp.sum(expo * dprob, axis=0, keepdims=True))
    top = functools.reduce(jnp.maximum, tops)
    shares = [jnp.exp(t - top) for t in tops]
    total = sum(s * t for s, t in zip(shares, totals))
    weight = sum(s * w for s, w in zip(shares, weights))
    stats = jnp.concatenate([top, total, weight], axis=0)
    out_ref[...] = jnp.broadcast_to(stats[None], out_ref.shape)


def chunk_ids(chips, y, core):
    step = 1 - 2 * core
    near, middle, far = (2 * lax.rem(y + n * step + chips, chips) for n in (1, 2, 3))
    across, same, other = 2 * lax.rem(y + chips // 2, chips), core, 1 - core
    return [
        near + same,
        far + same,
        far + other,
        near + other,
        middle + same,
        middle + other,
        across + same,
        2 * y + same,
    ]


def half_step(chunk, start, row_ref, target_ref, lat_ref, up_ref, book_ref):
    lat, up = lat_ref[...], up_ref[...]
    book = book_ref[pl.ds(start, chunk), :]
    scores = dot(book, lat, ROW_CONTRACT)
    dprob = dot(book, up, ROW_CONTRACT)
    probs = jnp.exp(scores - row_ref[0:1, :]) * row_ref[1:2, :]
    soft = probs * (dprob + row_ref[2:3, :])
    codes = lax.broadcasted_iota(jnp.int32, soft.shape, 0)
    dscore = jnp.where(codes == target_ref[...] - start, soft - 1.0, soft).astype(jnp.bfloat16)
    return dscore, dot(dscore, lat, PLAIN) + dot(probs.astype(jnp.bfloat16), up, PLAIN)


def away_kernel(chunk, ids_ref, row_ref, target_ref, lat_ref, up_ref, book_ref, grad_ref, dscore_ref):
    half = grad_ref.shape[0] // chunk
    for n in range(half):
        start = pl.multiple_of(ids_ref[half + n] * chunk, chunk)
        here = slice(n * chunk, (n + 1) * chunk)
        dscore_ref[here, :], grad_ref[here, :] = half_step(
            chunk, start, row_ref, target_ref, lat_ref, up_ref, book_ref
        )


def mine_kernel(
    chunk, ids_ref, row_ref, target_ref, lat_ref, up_ref, book_ref, away_ref, grad_ref, out_ref
):
    total = jnp.zeros((book_ref.shape[1], lat_ref.shape[0]), jnp.float32)
    half = grad_ref.shape[0] // chunk
    for n in range(half):
        start = pl.multiple_of(ids_ref[n] * chunk, chunk)
        away_start = pl.multiple_of(ids_ref[half + n] * chunk, chunk)
        here = slice(n * chunk, (n + 1) * chunk)
        dscore, grad_ref[here, :] = half_step(
            chunk, start, row_ref, target_ref, lat_ref, up_ref, book_ref
        )
        total += dot(book_ref[pl.ds(start, chunk), :], dscore, CODE_CONTRACT)
        total += dot(book_ref[pl.ds(away_start, chunk), :], away_ref[here, :], CODE_CONTRACT)
    out_ref[...] = total.T


def merge_kernel(chunk, middle_ref, ahead_ref, across_ref, same_ref, cross_ref):
    same_ref[...] = middle_ref[:chunk, :] + ahead_ref[chunk : 2 * chunk, :] + across_ref[...]
    cross_ref[...] = middle_ref[chunk:, :] + ahead_ref[2 * chunk :, :]


def hand_over_kernel(in_ref, out_ref):
    out_ref[...] = in_ref[...]


def shards(latents, upstream, targets, codebook):
    rows, width = latents.shape
    local_codes = codebook.shape[0]
    n_code = lax.axis_size("code")
    n_dp = lax.axis_size("dp")
    chips = n_dp // 2
    chunk = local_codes // n_dp
    here = lax.axis_index("dp")
    y, core = here // 2, lax.rem(here, 2)
    macs = rows * local_codes * width
    f32, bf16 = jnp.float32, jnp.bfloat16

    tile = 1024
    stats = pl.pallas_call(
        functools.partial(stats_kernel, tile),
        out_shape=jax.ShapeDtypeStruct((n_code, 3, rows), f32),
        in_specs=[HBM] * 3,
        out_specs=VMEM,
        scratch_shapes=[
            pltpu.VMEM((rows, width), bf16),
            pltpu.VMEM((rows, width), bf16),
            pltpu.VMEM((local_codes, width), bf16),
            pltpu.SemaphoreType.DMA((local_codes // tile + 2,)),
        ],
        compiler_params=pltpu.CompilerParams(vmem_limit_bytes=60 * 1024 * 1024),
        cost_estimate=pl.CostEstimate(
            flops=4 * macs, bytes_accessed=3 << 20, transcendentals=rows * local_codes
        ),
        name="stats",
    )(latents, upstream, codebook)
    every = lax.all_to_all(stats, "code", 0, 0)
    tops = every[:, 0]
    top = jnp.max(tops, axis=0)
    share = jnp.exp(tops - top[None])
    total = jnp.sum(share * every[:, 1], axis=0)
    rowdot = jnp.sum(share * every[:, 2], axis=0) / total
    row = jnp.stack([top, 1.0 / total, 1.0 - rowdot])
    local_target = (targets - lax.axis_index("code") * local_codes)[None]

    ids = jnp.stack(chunk_ids(chips, y, core) + chunk_ids(chips, y, 1 - core))
    operands = (ids, row, local_target, latents, upstream, codebook)
    away, away_dscore = pl.pallas_call(
        functools.partial(away_kernel, chunk),
        out_shape=(
            jax.ShapeDtypeStruct((local_codes // 2, width), f32),
            jax.ShapeDtypeStruct((local_codes // 2, rows), bf16),
        ),
        in_specs=[SMEM] + [VMEM] * 5,
        out_specs=(VMEM, VMEM),
        compiler_params=PARAMS,
        cost_estimate=pl.CostEstimate(
            flops=4 * macs, bytes_accessed=6 << 20, transcendentals=rows * local_codes // 2
        ),
        name="away_half",
    )(*operands)
    got = lax.ppermute(away, "dp", [(i, i ^ 1) for i in range(n_dp)])
    half, lat_part = pl.pallas_call(
        functools.partial(mine_kernel, chunk),
        out_shape=(
            jax.ShapeDtypeStruct((local_codes // 2, width), f32),
            jax.ShapeDtypeStruct((rows, width), f32),
        ),
        in_specs=[SMEM] + [VMEM] * 6,
        out_specs=(VMEM, VMEM),
        compiler_params=PARAMS,
        cost_estimate=pl.CostEstimate(
            flops=6 * macs, bytes_accessed=7 << 20, transcendentals=rows * local_codes // 2
        ),
        name="mine_half",
    )(*operands, away_dscore)

    def along(far, other=0):
        return [
            (i, (i // 2 + far * (1 - 2 * (i % 2))) % chips * 2 + (i + other) % 2)
            for i in range(n_dp)
        ]

    ahead, near_other, middle, across, own = [
        half[at * chunk : to * chunk] + got[at * chunk : to * chunk]
        for at, to in ((0, 3), (3, 4), (4, 6), (6, 7), (7, 8))
    ]
    ahead, near_other, middle, across, own, lat_part = lax.optimization_barrier(
        (ahead, near_other, middle, across, own, lat_part)
    )
    ahead_came = lax.ppermute(ahead, "dp", along(1))
    across_came = lax.ppermute(across, "dp", along(2))
    other_came = lax.ppermute(near_other, "dp", along(1, 1))
    merged = pl.pallas_call(
        functools.partial(merge_kernel, chunk),
        out_shape=[jax.ShapeDtypeStruct((chunk, width), f32)] * 2,
        in_specs=[VMEM] * 3,
        out_specs=[VMEM] * 2,
        compiler_params=PARAMS,
        cost_estimate=pl.CostEstimate(flops=12000000000, bytes_accessed=2 << 20, transcendentals=0),
        name="merge",
    )(middle, ahead_came, across_came)
    merged_came = [lax.ppermute(merged[n], "dp", along(2, n)) for n in (0, 1)]

    pieces = lax.all_to_all(lat_part.reshape(n_code, rows // n_code, width), "code", 0, 0)
    piece = jnp.sum(pieces, axis=0)
    latent_grad = lax.all_to_all(
        jnp.broadcast_to(piece[None], (n_code,) + piece.shape), "code", 0, 0
    ).reshape(rows, width)

    early = ahead_came[:chunk] + other_came + own
    latent_grad = pl.pallas_call(
        hand_over_kernel,
        out_shape=pltpu.HBM((rows, width), f32),
        in_specs=[VMEM],
        out_specs=VMEM,
        compiler_params=PARAMS,
        cost_estimate=pl.CostEstimate(flops=0, bytes_accessed=1 << 20, transcendentals=0),
        name="hand_over",
    )(latent_grad)
    latent_grad, early = lax.optimization_barrier((latent_grad, early))
    codebook_grad = early + merged_came[0] + merged_came[1]
    return (latent_grad, codebook_grad)


def solution(mesh):
    return jax.shard_map(
        shards,
        mesh=mesh,
        in_specs=(P("dp", None), P("dp", None), P("dp"), P("code", None)),
        out_specs=(P("dp", None), P(("code", "dp"), None)),
        check_vma=False,
    )
```

```python
import functools

import jax
import jax.numpy as jnp
from jax import lax
from jax.experimental import pallas as pl
from jax.experimental.pallas import tpu as pltpu
from jax.sharding import PartitionSpec as P

ROW_CONTRACT = (((1,), (1,)), ((), ()))
CODE_CONTRACT = (((0,), (0,)), ((), ()))
PLAIN = (((1,), (0,)), ((), ()))
VMEM = pl.BlockSpec(memory_space=pltpu.VMEM)
SMEM = pl.BlockSpec(memory_space=pltpu.SMEM)
HBM = pl.BlockSpec(memory_space=pltpu.HBM)
PARAMS = pltpu.CompilerParams(vmem_limit_bytes=24 * 1024 * 1024)


def dot(a, b, contract):
    return lax.dot_general(a, b, contract, preferred_element_type=jnp.float32)


def stats_kernel(edges, lat_hbm, up_hbm, book_hbm, out_ref, lat_ref, up_ref, book_ref, sems):
    parts = [pl.ds(start, end - start) for start, end in zip(edges, edges[1:])]
    lat_load = pltpu.make_async_copy(lat_hbm, lat_ref, sems.at[len(parts)])
    up_load = pltpu.make_async_copy(up_hbm, up_ref, sems.at[len(parts) + 1])
    loads = [
        pltpu.make_async_copy(book_hbm.at[part], book_ref.at[part], sems.at[n])
        for n, part in enumerate(parts)
    ]
    for load in (lat_load, loads[0], up_load, *loads[1:]):
        load.start()
    lat_load.wait()
    tops, totals, weights = [], [], []
    for n, part in enumerate(parts):
        loads[n].wait()
        book = book_ref[part, :]
        scores = dot(book, lat_ref[...], ROW_CONTRACT)
        if n == 0:
            up_load.wait()
        dprob = dot(book, up_ref[...], ROW_CONTRACT)
        top = jnp.max(scores, axis=0, keepdims=True)
        expo = jnp.exp(scores - top)
        tops.append(top)
        totals.append(jnp.sum(expo, axis=0, keepdims=True))
        weights.append(jnp.sum(expo * dprob, axis=0, keepdims=True))
    top = functools.reduce(jnp.maximum, tops)
    shares = [jnp.exp(t - top) for t in tops]
    total = sum(s * t for s, t in zip(shares, totals))
    weight = sum(s * w for s, w in zip(shares, weights))
    stats = jnp.concatenate([top, total, weight], axis=0)
    out_ref[...] = jnp.broadcast_to(stats[None], out_ref.shape)


def chunk_ids(chips, y, core):
    step = 1 - 2 * core
    near, middle, far = (2 * lax.rem(y + n * step + chips, chips) for n in (1, 2, 3))
    across, same, other = 2 * lax.rem(y + chips // 2, chips), core, 1 - core
    return [
        near + same,
        far + same,
        far + other,
        near + other,
        middle + same,
        middle + other,
        across + same,
        2 * y + same,
    ]


def half_step(chunk, start, row_ref, target_ref, lat_ref, up_ref, book_ref):
    lat, up = lat_ref[...], up_ref[...]
    book = book_ref[pl.ds(start, chunk), :]
    scores = dot(book, lat, ROW_CONTRACT)
    dprob = dot(book, up, ROW_CONTRACT)
    probs = jnp.exp(scores - row_ref[0:1, :]) * row_ref[1:2, :]
    soft = probs * (dprob + row_ref[2:3, :])
    codes = lax.broadcasted_iota(jnp.int32, soft.shape, 0)
    dscore = jnp.where(codes == target_ref[...] - start, soft - 1.0, soft).astype(jnp.bfloat16)
    return dscore, dot(dscore, lat, PLAIN) + dot(probs.astype(jnp.bfloat16), up, PLAIN)


def away_kernel(chunk, ids_ref, row_ref, target_ref, lat_ref, up_ref, book_ref, grad_ref, dscore_ref):
    half = grad_ref.shape[0] // chunk
    for n in range(half):
        start = pl.multiple_of(ids_ref[half + n] * chunk, chunk)
        here = slice(n * chunk, (n + 1) * chunk)
        dscore_ref[here, :], grad_ref[here, :] = half_step(
            chunk, start, row_ref, target_ref, lat_ref, up_ref, book_ref
        )


def mine_kernel(
    chunk, ids_ref, row_ref, target_ref, lat_ref, up_ref, book_ref, away_ref, grad_ref, out_ref
):
    half = grad_ref.shape[0] // chunk
    books, away_books, dscores = [], [], []
    for n in range(half):
        start = pl.multiple_of(ids_ref[n] * chunk, chunk)
        away_start = pl.multiple_of(ids_ref[half + n] * chunk, chunk)
        here = slice(n * chunk, (n + 1) * chunk)
        dscore, grad_ref[here, :] = half_step(
            chunk, start, row_ref, target_ref, lat_ref, up_ref, book_ref
        )
        books.append(book_ref[pl.ds(start, chunk), :])
        away_books.append(book_ref[pl.ds(away_start, chunk), :])
        dscores.append(dscore)
    total = dot(jnp.concatenate(books), jnp.concatenate(dscores), CODE_CONTRACT)
    total += dot(jnp.concatenate(away_books), away_ref[...], CODE_CONTRACT)
    out_ref[...] = total.T


def merge_kernel(chunk, middle_ref, ahead_ref, across_ref, same_ref, cross_ref):
    same_ref[...] = middle_ref[:chunk, :] + ahead_ref[chunk : 2 * chunk, :] + across_ref[...]
    cross_ref[...] = middle_ref[chunk:, :] + ahead_ref[2 * chunk :, :]


def hand_over_kernel(in_ref, out_ref):
    out_ref[...] = in_ref[...]


def shards(latents, upstream, targets, codebook):
    rows, width = latents.shape
    local_codes = codebook.shape[0]
    n_code = lax.axis_size("code")
    n_dp = lax.axis_size("dp")
    chips = n_dp // 2
    chunk = local_codes // n_dp
    here = lax.axis_index("dp")
    y, core = here // 2, lax.rem(here, 2)
    macs = rows * local_codes * width
    f32, bf16 = jnp.float32, jnp.bfloat16

    edges = (0, chunk, local_codes // 2, local_codes)
    stats = pl.pallas_call(
        functools.partial(stats_kernel, edges),
        out_shape=jax.ShapeDtypeStruct((n_code, 3, rows), f32),
        in_specs=[HBM] * 3,
        out_specs=VMEM,
        scratch_shapes=[
            pltpu.VMEM((rows, width), bf16),
            pltpu.VMEM((rows, width), bf16),
            pltpu.VMEM((local_codes, width), bf16),
            pltpu.SemaphoreType.DMA((len(edges) + 1,)),
        ],
        compiler_params=pltpu.CompilerParams(vmem_limit_bytes=60 * 1024 * 1024),
        cost_estimate=pl.CostEstimate(
            flops=4 * macs, bytes_accessed=3 << 20, transcendentals=rows * local_codes
        ),
        name="stats",
    )(latents, upstream, codebook)
    every = lax.all_to_all(stats, "code", 0, 0)
    tops = every[:, 0]
    top = jnp.max(tops, axis=0)
    share = jnp.exp(tops - top[None])
    total = jnp.sum(share * every[:, 1], axis=0)
    rowdot = jnp.sum(share * every[:, 2], axis=0) / total
    row = jnp.stack([top, 1.0 / total, 1.0 - rowdot])
    local_target = (targets - lax.axis_index("code") * local_codes)[None]

    ids = jnp.stack(chunk_ids(chips, y, core) + chunk_ids(chips, y, 1 - core))
    operands = (ids, row, local_target, latents, upstream, codebook)
    away, away_dscore = pl.pallas_call(
        functools.partial(away_kernel, chunk),
        out_shape=(
            jax.ShapeDtypeStruct((local_codes // 2, width), f32),
            jax.ShapeDtypeStruct((local_codes // 2, rows), bf16),
        ),
        in_specs=[SMEM] + [VMEM] * 5,
        out_specs=(VMEM, VMEM),
        compiler_params=PARAMS,
        cost_estimate=pl.CostEstimate(
            flops=4 * macs, bytes_accessed=6 << 20, transcendentals=rows * local_codes // 2
        ),
        name="away_half",
    )(*operands)
    got = lax.ppermute(away, "dp", [(i, i ^ 1) for i in range(n_dp)])
    half, lat_part = pl.pallas_call(
        functools.partial(mine_kernel, chunk),
        out_shape=(
            jax.ShapeDtypeStruct((local_codes // 2, width), f32),
            jax.ShapeDtypeStruct((rows, width), f32),
        ),
        in_specs=[SMEM] + [VMEM] * 6,
        out_specs=(VMEM, VMEM),
        compiler_params=PARAMS,
        cost_estimate=pl.CostEstimate(
            flops=6 * macs, bytes_accessed=7 << 20, transcendentals=rows * local_codes // 2
        ),
        name="mine_half",
    )(*operands, away_dscore)

    def along(far, other=0):
        return [
            (i, (i // 2 + far * (1 - 2 * (i % 2))) % chips * 2 + (i + other) % 2)
            for i in range(n_dp)
        ]

    ahead, near_other, middle, across, own = [
        half[at * chunk : to * chunk] + got[at * chunk : to * chunk]
        for at, to in ((0, 3), (3, 4), (4, 6), (6, 7), (7, 8))
    ]
    ahead, near_other, middle, across, own, lat_part = lax.optimization_barrier(
        (ahead, near_other, middle, across, own, lat_part)
    )
    ahead_came = lax.ppermute(ahead, "dp", along(1))
    across_came = lax.ppermute(across, "dp", along(2))
    other_came = lax.ppermute(near_other, "dp", along(1, 1))
    merged = pl.pallas_call(
        functools.partial(merge_kernel, chunk),
        out_shape=[jax.ShapeDtypeStruct((chunk, width), f32)] * 2,
        in_specs=[VMEM] * 3,
        out_specs=[VMEM] * 2,
        compiler_params=PARAMS,
        cost_estimate=pl.CostEstimate(flops=12000000000, bytes_accessed=2 << 20, transcendentals=0),
        name="merge",
    )(middle, ahead_came, across_came)
    merged_came = [lax.ppermute(merged[n], "dp", along(2, n)) for n in (0, 1)]

    pieces = lax.all_to_all(lat_part.reshape(n_code, rows // n_code, width), "code", 0, 0)
    piece = jnp.sum(pieces, axis=0)
    latent_grad = lax.all_to_all(
        jnp.broadcast_to(piece[None], (n_code,) + piece.shape), "code", 0, 0
    ).reshape(rows, width)

    early = ahead_came[:chunk] + other_came + own
    latent_grad = pl.pallas_call(
        hand_over_kernel,
        out_shape=pltpu.HBM((rows, width), f32),
        in_specs=[VMEM],
        out_specs=VMEM,
        compiler_params=PARAMS,
        cost_estimate=pl.CostEstimate(flops=0, bytes_accessed=1 << 20, transcendentals=0),
        name="hand_over",
    )(latent_grad)
    latent_grad, early = lax.optimization_barrier((latent_grad, early))
    codebook_grad = early + merged_came[0] + merged_came[1]
    return (latent_grad, codebook_grad)


def solution(mesh):
    return jax.shard_map(
        shards,
        mesh=mesh,
        in_specs=(P("dp", None), P("dp", None), P("dp"), P("code", None)),
        out_specs=(P("dp", None), P(("code", "dp"), None)),
        check_vma=False,
    )
```

```python
import functools

import jax
import jax.numpy as jnp
from jax import lax
from jax.experimental import pallas as pl
from jax.experimental.pallas import tpu as pltpu
from jax.sharding import PartitionSpec as P

ROW_CONTRACT = (((1,), (1,)), ((), ()))
CODE_CONTRACT = (((0,), (0,)), ((), ()))
PLAIN = (((1,), (0,)), ((), ()))
VMEM = pl.BlockSpec(memory_space=pltpu.VMEM)
SMEM = pl.BlockSpec(memory_space=pltpu.SMEM)
HBM = pl.BlockSpec(memory_space=pltpu.HBM)
PARAMS = pltpu.CompilerParams(vmem_limit_bytes=24 * 1024 * 1024)


def dot(a, b, contract):
    return lax.dot_general(a, b, contract, preferred_element_type=jnp.float32)


def stats_kernel(edges, lat_hbm, up_hbm, book_hbm, out_ref, lat_ref, up_ref, book_ref, sems):
    parts = [pl.ds(start, end - start) for start, end in zip(edges, edges[1:])]
    lat_load = pltpu.make_async_copy(lat_hbm, lat_ref, sems.at[len(parts)])
    up_load = pltpu.make_async_copy(up_hbm, up_ref, sems.at[len(parts) + 1])
    loads = [
        pltpu.make_async_copy(book_hbm.at[part], book_ref.at[part], sems.at[n])
        for n, part in enumerate(parts)
    ]
    for load in (lat_load, loads[0], up_load, *loads[1:]):
        load.start()
    lat_load.wait()
    tops, totals, weights = [], [], []
    for n, part in enumerate(parts):
        loads[n].wait()
        book = book_ref[part, :]
        scores = dot(book, lat_ref[...], ROW_CONTRACT)
        if n == 0:
            up_load.wait()
        dprob = dot(book, up_ref[...], ROW_CONTRACT)
        top = jnp.max(scores, axis=0, keepdims=True)
        expo = jnp.exp(scores - top)
        tops.append(top)
        totals.append(jnp.sum(expo, axis=0, keepdims=True))
        weights.append(jnp.sum(expo * dprob, axis=0, keepdims=True))
    top = functools.reduce(jnp.maximum, tops)
    shares = [jnp.exp(t - top) for t in tops]
    total = sum(s * t for s, t in zip(shares, totals))
    weight = sum(s * w for s, w in zip(shares, weights))
    stats = jnp.concatenate([top, total, weight], axis=0)
    out_ref[...] = jnp.broadcast_to(stats[None], out_ref.shape)


def chunk_ids(chips, y, core):
    step = 1 - 2 * core
    near, middle, far = (2 * lax.rem(y + n * step + chips, chips) for n in (1, 2, 3))
    across, same, other = 2 * lax.rem(y + chips // 2, chips), core, 1 - core
    return [
        near + same,
        far + same,
        far + other,
        near + other,
        middle + same,
        middle + other,
        across + same,
        2 * y + same,
    ]


def half_step(chunk, start, row_ref, target_ref, lat_ref, up_ref, book_ref):
    lat, up = lat_ref[...], up_ref[...]
    book = book_ref[pl.ds(start, chunk), :]
    scores = dot(book, lat, ROW_CONTRACT)
    dprob = dot(book, up, ROW_CONTRACT)
    probs = jnp.exp(scores - row_ref[0:1, :]) * row_ref[1:2, :]
    soft = probs * (dprob + row_ref[2:3, :])
    codes = lax.broadcasted_iota(jnp.int32, soft.shape, 0)
    dscore = jnp.where(codes == target_ref[...] - start, soft - 1.0, soft).astype(jnp.bfloat16)
    return dscore, dot(dscore, lat, PLAIN) + dot(probs.astype(jnp.bfloat16), up, PLAIN)


def away_kernel(chunk, ids_ref, row_ref, target_ref, lat_ref, up_ref, book_ref, grad_ref, dscore_ref):
    half = grad_ref.shape[0] // chunk
    for n in range(half):
        start = pl.multiple_of(ids_ref[half + n] * chunk, chunk)
        here = slice(n * chunk, (n + 1) * chunk)
        dscore_ref[here, :], grad_ref[here, :] = half_step(
            chunk, start, row_ref, target_ref, lat_ref, up_ref, book_ref
        )


def mine_kernel(
    chunk, ids_ref, row_ref, target_ref, lat_ref, up_ref, book_ref, away_ref, grad_ref, out_ref
):
    half = grad_ref.shape[0] // chunk
    books, away_books, dscores = [], [], []
    for n in range(half):
        start = pl.multiple_of(ids_ref[n] * chunk, chunk)
        away_start = pl.multiple_of(ids_ref[half + n] * chunk, chunk)
        here = slice(n * chunk, (n + 1) * chunk)
        dscore, grad_ref[here, :] = half_step(
            chunk, start, row_ref, target_ref, lat_ref, up_ref, book_ref
        )
        books.append(book_ref[pl.ds(start, chunk), :])
        away_books.append(book_ref[pl.ds(away_start, chunk), :])
        dscores.append(dscore)
    total = dot(jnp.concatenate(books), jnp.concatenate(dscores), CODE_CONTRACT)
    total += dot(jnp.concatenate(away_books), away_ref[...], CODE_CONTRACT)
    out_ref[...] = total.T


def merge_kernel(chunk, middle_ref, ahead_ref, across_ref, same_ref, cross_ref):
    same_ref[...] = middle_ref[:chunk, :] + ahead_ref[chunk : 2 * chunk, :] + across_ref[...]
    cross_ref[...] = middle_ref[chunk:, :] + ahead_ref[2 * chunk :, :]


def hand_over_kernel(in_ref, out_ref):
    out_ref[...] = in_ref[...]


def shards(latents, upstream, targets, codebook):
    rows, width = latents.shape
    local_codes = codebook.shape[0]
    n_code = lax.axis_size("code")
    n_dp = lax.axis_size("dp")
    chips = n_dp // 2
    chunk = local_codes // n_dp
    here = lax.axis_index("dp")
    y, core = here // 2, lax.rem(here, 2)
    macs = rows * local_codes * width
    f32, bf16 = jnp.float32, jnp.bfloat16

    edges = (0, chunk, local_codes // 2, local_codes)
    stats, lat_held, up_held, book_held = pl.pallas_call(
        functools.partial(stats_kernel, edges),
        out_shape=(
            jax.ShapeDtypeStruct((n_code, 3, rows), f32),
            pltpu.VMEM((rows, width), bf16),
            pltpu.VMEM((rows, width), bf16),
            pltpu.VMEM((local_codes, width), bf16),
        ),
        in_specs=[HBM] * 3,
        out_specs=(VMEM,) * 4,
        scratch_shapes=[pltpu.SemaphoreType.DMA((len(edges) + 1,))],
        compiler_params=pltpu.CompilerParams(vmem_limit_bytes=60 * 1024 * 1024),
        cost_estimate=pl.CostEstimate(
            flops=4 * macs, bytes_accessed=3 << 20, transcendentals=rows * local_codes
        ),
        name="stats",
    )(latents, upstream, codebook)
    every = lax.all_to_all(stats, "code", 0, 0)
    tops = every[:, 0]
    top = jnp.max(tops, axis=0)
    share = jnp.exp(tops - top[None])
    total = jnp.sum(share * every[:, 1], axis=0)
    rowdot = jnp.sum(share * every[:, 2], axis=0) / total
    row = jnp.stack([top, 1.0 / total, 1.0 - rowdot])
    local_target = (targets - lax.axis_index("code") * local_codes)[None]

    ids = jnp.stack(chunk_ids(chips, y, core) + chunk_ids(chips, y, 1 - core))
    operands = (ids, row, local_target, lat_held, up_held, book_held)
    away, away_dscore = pl.pallas_call(
        functools.partial(away_kernel, chunk),
        out_shape=(
            jax.ShapeDtypeStruct((local_codes // 2, width), f32),
            jax.ShapeDtypeStruct((local_codes // 2, rows), bf16),
        ),
        in_specs=[SMEM] + [VMEM] * 5,
        out_specs=(VMEM, VMEM),
        compiler_params=PARAMS,
        cost_estimate=pl.CostEstimate(
            flops=4 * macs, bytes_accessed=6 << 20, transcendentals=rows * local_codes // 2
        ),
        name="away_half",
    )(*operands)
    got = lax.ppermute(away, "dp", [(i, i ^ 1) for i in range(n_dp)])
    half, lat_part = pl.pallas_call(
        functools.partial(mine_kernel, chunk),
        out_shape=(
            jax.ShapeDtypeStruct((local_codes // 2, width), f32),
            jax.ShapeDtypeStruct((rows, width), f32),
        ),
        in_specs=[SMEM] + [VMEM] * 6,
        out_specs=(VMEM, VMEM),
        compiler_params=PARAMS,
        cost_estimate=pl.CostEstimate(
            flops=6 * macs, bytes_accessed=7 << 20, transcendentals=rows * local_codes // 2
        ),
        name="mine_half",
    )(*operands, away_dscore)

    def along(far, other=0):
        return [
            (i, (i // 2 + far * (1 - 2 * (i % 2))) % chips * 2 + (i + other) % 2)
            for i in range(n_dp)
        ]

    ahead, near_other, middle, across, own = [
        half[at * chunk : to * chunk] + got[at * chunk : to * chunk]
        for at, to in ((0, 3), (3, 4), (4, 6), (6, 7), (7, 8))
    ]
    ahead, near_other, middle, across, own, lat_part = lax.optimization_barrier(
        (ahead, near_other, middle, across, own, lat_part)
    )
    ahead_came = lax.ppermute(ahead, "dp", along(1))
    across_came = lax.ppermute(across, "dp", along(2))
    other_came = lax.ppermute(near_other, "dp", along(1, 1))
    merged = pl.pallas_call(
        functools.partial(merge_kernel, chunk),
        out_shape=[jax.ShapeDtypeStruct((chunk, width), f32)] * 2,
        in_specs=[VMEM] * 3,
        out_specs=[VMEM] * 2,
        compiler_params=PARAMS,
        cost_estimate=pl.CostEstimate(flops=12000000000, bytes_accessed=2 << 20, transcendentals=0),
        name="merge",
    )(middle, ahead_came, across_came)
    merged_came = [lax.ppermute(merged[n], "dp", along(2, n)) for n in (0, 1)]

    pieces = lax.all_to_all(lat_part.reshape(n_code, rows // n_code, width), "code", 0, 0)
    piece = jnp.sum(pieces, axis=0)
    latent_grad = lax.all_to_all(
        jnp.broadcast_to(piece[None], (n_code,) + piece.shape), "code", 0, 0
    ).reshape(rows, width)

    early = ahead_came[:chunk] + other_came + own
    latent_grad = pl.pallas_call(
        hand_over_kernel,
        out_shape=pltpu.HBM((rows, width), f32),
        in_specs=[VMEM],
        out_specs=VMEM,
        compiler_params=PARAMS,
        cost_estimate=pl.CostEstimate(flops=0, bytes_accessed=1 << 20, transcendentals=0),
        name="hand_over",
    )(latent_grad)
    latent_grad, early = lax.optimization_barrier((latent_grad, early))
    codebook_grad = early + merged_came[0] + merged_came[1]
    return (latent_grad, codebook_grad)


def solution(mesh):
    return jax.shard_map(
        shards,
        mesh=mesh,
        in_specs=(P("dp", None), P("dp", None), P("dp"), P("code", None)),
        out_specs=(P("dp", None), P(("code", "dp"), None)),
        check_vma=False,
    )
```

```python
import functools

import jax
import jax.numpy as jnp
from jax import lax
from jax.experimental import pallas as pl
from jax.experimental.pallas import tpu as pltpu
from jax.sharding import PartitionSpec as P

ROW_CONTRACT = (((1,), (1,)), ((), ()))
CODE_CONTRACT = (((0,), (0,)), ((), ()))
PLAIN = (((1,), (0,)), ((), ()))
VMEM = pl.BlockSpec(memory_space=pltpu.VMEM)
SMEM = pl.BlockSpec(memory_space=pltpu.SMEM)
HBM = pl.BlockSpec(memory_space=pltpu.HBM)
PARAMS = pltpu.CompilerParams(vmem_limit_bytes=24 * 1024 * 1024)


def dot(a, b, contract):
    return lax.dot_general(a, b, contract, preferred_element_type=jnp.float32)


def stats_kernel(edges, lat_hbm, up_hbm, book_hbm, out_ref, lat_ref, up_ref, book_ref, sems):
    parts = [pl.ds(start, end - start) for start, end in zip(edges, edges[1:])]
    lat_load = pltpu.make_async_copy(lat_hbm, lat_ref, sems.at[len(parts)])
    up_load = pltpu.make_async_copy(up_hbm, up_ref, sems.at[len(parts) + 1])
    loads = [
        pltpu.make_async_copy(book_hbm.at[part], book_ref.at[part], sems.at[n])
        for n, part in enumerate(parts)
    ]
    for load in (lat_load, loads[0], up_load, *loads[1:]):
        load.start()
    lat_load.wait()
    tops, totals, weights = [], [], []
    for n, part in enumerate(parts):
        loads[n].wait()
        book = book_ref[part, :]
        scores = dot(book, lat_ref[...], ROW_CONTRACT)
        if n == 0:
            up_load.wait()
        dprob = dot(book, up_ref[...], ROW_CONTRACT)
        top = jnp.max(scores, axis=0, keepdims=True)
        expo = jnp.exp(scores - top)
        tops.append(top)
        totals.append(jnp.sum(expo, axis=0, keepdims=True))
        weights.append(jnp.sum(expo * dprob, axis=0, keepdims=True))
    top = functools.reduce(jnp.maximum, tops)
    shares = [jnp.exp(t - top) for t in tops]
    total = sum(s * t for s, t in zip(shares, totals))
    weight = sum(s * w for s, w in zip(shares, weights))
    stats = jnp.concatenate([top, total, weight], axis=0)
    out_ref[...] = jnp.broadcast_to(stats[None], out_ref.shape)


def chunk_ids(chips, y, core):
    step = 1 - 2 * core
    near, middle, far = (2 * lax.rem(y + n * step + chips, chips) for n in (1, 2, 3))
    across, same, other = 2 * lax.rem(y + chips // 2, chips), core, 1 - core
    return [
        near + same,
        far + same,
        far + other,
        near + other,
        middle + same,
        middle + other,
        across + same,
        2 * y + same,
    ]


def half_step(chunk, start, row_ref, target_ref, lat_ref, up_ref, book_ref):
    lat, up = lat_ref[...], up_ref[...]
    book = book_ref[pl.ds(start, chunk), :]
    scores = dot(book, lat, ROW_CONTRACT)
    dprob = dot(book, up, ROW_CONTRACT)
    probs = jnp.exp(scores - row_ref[0:1, :]) * row_ref[1:2, :]
    soft = probs * (dprob + row_ref[2:3, :])
    codes = lax.broadcasted_iota(jnp.int32, soft.shape, 0)
    dscore = jnp.where(codes == target_ref[...] - start, soft - 1.0, soft).astype(jnp.bfloat16)
    return dscore, dot(dscore, lat, PLAIN) + dot(probs.astype(jnp.bfloat16), up, PLAIN)


def away_kernel(chunk, ids_ref, row_ref, target_ref, lat_ref, up_ref, book_ref, grad_ref, dscore_ref):
    half = grad_ref.shape[0] // chunk
    for n in range(half):
        start = pl.multiple_of(ids_ref[half + n] * chunk, chunk)
        here = slice(n * chunk, (n + 1) * chunk)
        dscore_ref[here, :], grad_ref[here, :] = half_step(
            chunk, start, row_ref, target_ref, lat_ref, up_ref, book_ref
        )


def mine_kernel(
    chunk, ids_ref, row_ref, target_ref, lat_ref, up_ref, book_ref, away_ref, grad_ref, out_ref
):
    half = grad_ref.shape[0] // chunk
    books, dscores = [], []
    away_starts = [pl.multiple_of(ids_ref[half + n] * chunk, chunk) for n in range(half)]
    away_books = [book_ref[pl.ds(start, chunk), :] for start in away_starts]
    total = dot(jnp.concatenate(away_books), away_ref[...], CODE_CONTRACT)
    for n in range(half):
        start = pl.multiple_of(ids_ref[n] * chunk, chunk)
        here = slice(n * chunk, (n + 1) * chunk)
        dscore, grad_ref[here, :] = half_step(
            chunk, start, row_ref, target_ref, lat_ref, up_ref, book_ref
        )
        books.append(book_ref[pl.ds(start, chunk), :])
        dscores.append(dscore)
    total += dot(jnp.concatenate(books), jnp.concatenate(dscores), CODE_CONTRACT)
    out_ref[...] = total.T


def merge_kernel(chunk, middle_ref, ahead_ref, across_ref, same_ref, cross_ref):
    same_ref[...] = middle_ref[:chunk, :] + ahead_ref[chunk : 2 * chunk, :] + across_ref[...]
    cross_ref[...] = middle_ref[chunk:, :] + ahead_ref[2 * chunk :, :]


def hand_over_kernel(in_ref, out_ref):
    out_ref[...] = in_ref[...]


def shards(latents, upstream, targets, codebook):
    rows, width = latents.shape
    local_codes = codebook.shape[0]
    n_code = lax.axis_size("code")
    n_dp = lax.axis_size("dp")
    chips = n_dp // 2
    chunk = local_codes // n_dp
    here = lax.axis_index("dp")
    y, core = here // 2, lax.rem(here, 2)
    macs = rows * local_codes * width
    f32, bf16 = jnp.float32, jnp.bfloat16

    edges = (0, chunk, local_codes // 2, local_codes)
    stats, lat_held, up_held, book_held = pl.pallas_call(
        functools.partial(stats_kernel, edges),
        out_shape=(
            jax.ShapeDtypeStruct((n_code, 3, rows), f32),
            pltpu.VMEM((rows, width), bf16),
            pltpu.VMEM((rows, width), bf16),
            pltpu.VMEM((local_codes, width), bf16),
        ),
        in_specs=[HBM] * 3,
        out_specs=(VMEM,) * 4,
        scratch_shapes=[pltpu.SemaphoreType.DMA((len(edges) + 1,))],
        compiler_params=pltpu.CompilerParams(vmem_limit_bytes=60 * 1024 * 1024),
        cost_estimate=pl.CostEstimate(
            flops=4 * macs, bytes_accessed=3 << 20, transcendentals=rows * local_codes
        ),
        name="stats",
    )(latents, upstream, codebook)
    every = lax.all_to_all(stats, "code", 0, 0)
    tops = every[:, 0]
    top = jnp.max(tops, axis=0)
    share = jnp.exp(tops - top[None])
    total = jnp.sum(share * every[:, 1], axis=0)
    rowdot = jnp.sum(share * every[:, 2], axis=0) / total
    row = jnp.stack([top, 1.0 / total, 1.0 - rowdot])
    local_target = (targets - lax.axis_index("code") * local_codes)[None]

    ids = jnp.stack(chunk_ids(chips, y, core) + chunk_ids(chips, y, 1 - core))
    operands = (ids, row, local_target, lat_held, up_held, book_held)
    away, away_dscore = pl.pallas_call(
        functools.partial(away_kernel, chunk),
        out_shape=(
            jax.ShapeDtypeStruct((local_codes // 2, width), f32),
            jax.ShapeDtypeStruct((local_codes // 2, rows), bf16),
        ),
        in_specs=[SMEM] + [VMEM] * 5,
        out_specs=(VMEM, VMEM),
        compiler_params=PARAMS,
        cost_estimate=pl.CostEstimate(
            flops=4 * macs, bytes_accessed=6 << 20, transcendentals=rows * local_codes // 2
        ),
        name="away_half",
    )(*operands)
    got = lax.ppermute(away, "dp", [(i, i ^ 1) for i in range(n_dp)])
    half, lat_part = pl.pallas_call(
        functools.partial(mine_kernel, chunk),
        out_shape=(
            jax.ShapeDtypeStruct((local_codes // 2, width), f32),
            jax.ShapeDtypeStruct((rows, width), f32),
        ),
        in_specs=[SMEM] + [VMEM] * 6,
        out_specs=(VMEM, VMEM),
        compiler_params=PARAMS,
        cost_estimate=pl.CostEstimate(
            flops=6 * macs, bytes_accessed=7 << 20, transcendentals=rows * local_codes // 2
        ),
        name="mine_half",
    )(*operands, away_dscore)

    def along(far, other=0):
        return [
            (i, (i // 2 + far * (1 - 2 * (i % 2))) % chips * 2 + (i + other) % 2)
            for i in range(n_dp)
        ]

    ahead, near_other, middle, across, own = [
        half[at * chunk : to * chunk] + got[at * chunk : to * chunk]
        for at, to in ((0, 3), (3, 4), (4, 6), (6, 7), (7, 8))
    ]
    ahead, near_other, middle, across, own, lat_part = lax.optimization_barrier(
        (ahead, near_other, middle, across, own, lat_part)
    )
    ahead_came = lax.ppermute(ahead, "dp", along(1))
    across_came = lax.ppermute(across, "dp", along(2))
    other_came = lax.ppermute(near_other, "dp", along(1, 1))
    merged = pl.pallas_call(
        functools.partial(merge_kernel, chunk),
        out_shape=[jax.ShapeDtypeStruct((chunk, width), f32)] * 2,
        in_specs=[VMEM] * 3,
        out_specs=[VMEM] * 2,
        compiler_params=PARAMS,
        cost_estimate=pl.CostEstimate(flops=12000000000, bytes_accessed=2 << 20, transcendentals=0),
        name="merge",
    )(middle, ahead_came, across_came)
    merged_came = [lax.ppermute(merged[n], "dp", along(2, n)) for n in (0, 1)]

    pieces = lax.all_to_all(lat_part.reshape(n_code, rows // n_code, width), "code", 0, 0)
    piece = jnp.sum(pieces, axis=0)
    latent_grad = lax.all_to_all(
        jnp.broadcast_to(piece[None], (n_code,) + piece.shape), "code", 0, 0
    ).reshape(rows, width)

    early = ahead_came[:chunk] + other_came + own
    latent_grad = pl.pallas_call(
        hand_over_kernel,
        out_shape=pltpu.HBM((rows, width), f32),
        in_specs=[VMEM],
        out_specs=VMEM,
        compiler_params=PARAMS,
        cost_estimate=pl.CostEstimate(flops=0, bytes_accessed=1 << 20, transcendentals=0),
        name="hand_over",
    )(latent_grad)
    latent_grad, early = lax.optimization_barrier((latent_grad, early))
    codebook_grad = early + merged_came[0] + merged_came[1]
    return (latent_grad, codebook_grad)


def solution(mesh):
    return jax.shard_map(
        shards,
        mesh=mesh,
        in_specs=(P("dp", None), P("dp", None), P("dp"), P("code", None)),
        out_specs=(P("dp", None), P(("code", "dp"), None)),
        check_vma=False,
    )
```
